32 devices in a mesh: head: 4 (over x, core), seq: 8 (over z, y).
Axes of the slice: x: 2, y: 2, z: 4, core: 2. Of those that a mesh axis runs over, the one named last changes fastest.
Arguments:
- x_input: bfloat16 [8192, 16384], P('seq', 'head'), may hold values from -5 to 5
- bc_input: bfloat16 [2, 8192, 1024], P(None, 'seq', 'head'), may hold values from -5 to 5
- dt_input: bfloat16 [8192, 128], P('seq', 'head'), may hold values from -8 to 256
- z_gate: bfloat16 [8192, 16384], P('seq', 'head'), may hold values from -400 to 400
- conv_x: float32 [4, 16384], P(None, 'head'), may hold values from -2 to 2
- conv_bc: float32 [2, 4, 1024], P(None, None, 'head'), may hold values from -2 to 2
- dt_bias: float32 [128], P('head'), may hold values from -0.3 to 0.3
- a_log: float32 [128], P('head'), may hold values from -10 to 1
- d_skip: float32 [128], P('head'), may hold values from 0.5 to 1.5
- init_state: float32 [128, 128, 128], P('head'), may hold values from -5 to 5
- norm_gain: float32 [16384], P('head'), may hold values from 0.5 to 1.5
Outputs:
- normed: bfloat16 [8192, 16384], P('seq', 'head')
The draws below stay inside these ranges and needn't reach their ends.
All inputs are finite; a program needn't handle non-finite values.
Results may differ from the reference program's by a relative error of at most 0.0034.
Values may be sent and summed in bfloat16 or wider, within the bound.
A program may use at most 128 MiB of HBM per device.

```python
import jax
import jax.numpy as jnp
from jax import lax

HEADS = 128
HDIM = 128
STATE = 128
GROUPS = 8
SPAN = 256
CONV = 4
TOK_DEV = 1024
INNER = 16384
WINDOW_TOKENS = 8192


def active_rows(key):
    subkey = jax.random.fold_in(key, 9001)
    token_slots = jax.random.randint(subkey, (2,), 8, WINDOW_TOKENS)
    token_position = jnp.arange(WINDOW_TOKENS)
    active_row = jnp.any(token_position[:, None] == token_slots[None, :], axis=1)
    silent_row = jnp.any((token_position[:, None] <= token_slots[None, :]) & (token_position[:, None] >= token_slots[None, :] - 3), axis=1)
    return (active_row, silent_row)


def draw_x_input(key, part):
    values = jnp.clip(jax.random.normal(jax.random.fold_in(key, 1), (WINDOW_TOKENS, INNER), jnp.float32), -5.0, 5.0)
    active_row, silent_row = active_rows(key)
    return jnp.where(silent_row[:, None], values / WINDOW_TOKENS, values).astype(jnp.bfloat16)


def draw_dt_input(key, part):
    noise = jnp.clip(jax.random.normal(jax.random.fold_in(key, 2), (WINDOW_TOKENS, HEADS), jnp.float32), -4.0, 4.0)
    offset = jax.random.uniform(jax.random.fold_in(key, 3), (WINDOW_TOKENS // TOK_DEV, 1, HEADS), jnp.float32, -0.7, 0.7)
    starting_offset = ((-4.0 + 0.7 * noise).reshape(WINDOW_TOKENS // TOK_DEV, TOK_DEV, HEADS) + offset).reshape(WINDOW_TOKENS, HEADS)
    active_row, silent_row = active_rows(key)
    return jnp.where(active_row[:, None], WINDOW_TOKENS / 32.0, starting_offset).astype(jnp.bfloat16)


def draw_a_log(key, part):
    share = 0.5
    fast_head = jax.random.uniform(jax.random.fold_in(key, 4), (HEADS,), jnp.float32) < share
    fast_rate = jax.random.uniform(jax.random.fold_in(key, 5), (HEADS,), jnp.float32, 1.0, 2.0)
    slow_log = jax.random.uniform(jax.random.fold_in(key, 6), (HEADS,), jnp.float32, jnp.log(0.13), jnp.log(0.45))
    slow_rate = jnp.exp(slow_log) / (0.02 * WINDOW_TOKENS)
    return jnp.log(jnp.where(fast_head, fast_rate, slow_rate))


def draw_z_gate(key, part):
    noise = jnp.clip(jax.random.normal(jax.random.fold_in(key, 7), (WINDOW_TOKENS, INNER), jnp.float32), -5.0, 5.0)
    column_scale = jnp.power(10.0, jax.random.uniform(jax.random.fold_in(key, 9), (INNER,), jnp.float32))
    column_scale = column_scale * (1.0 + 1.2 * jnp.arange(INNER, dtype=jnp.float32) / INNER)
    return (noise * column_scale).astype(jnp.bfloat16)


def steps_of(key, extent, split, least, high):
    loudness = 1.0
    for position, shards_of in split:
        heights = jax.random.uniform(jax.random.fold_in(jax.random.fold_in(key, 6), position), (shards_of,), jnp.float32, least / len(split), high / len(split))
        loudness = loudness * jnp.repeat(jnp.exp(heights), extent[position] // shards_of).reshape((-1,) + (1,) * (len(extent) - 1 - position))
    return loudness


def gaussian(rng, extent, spread, bound, cuts=(), kind=jnp.bfloat16):
    array = spread * jax.random.normal(rng, extent, jnp.float32)
    if cuts:
        array = array * steps_of(rng, extent, cuts, -0.22, 0.18)
    return jnp.clip(array, -bound, bound).astype(kind)


def setup_inputs(seed: int = 0) -> dict:
    key_list = jax.random.split(jax.random.key(seed), 12)
    x_input = draw_x_input(jax.random.fold_in(key_list[11], 71), 0)
    bc_input = gaussian(key_list[1], (2, WINDOW_TOKENS, GROUPS * STATE), 1.0, 5.0, ((1, 8), (2, 4)))
    dt_input = draw_dt_input(jax.random.fold_in(key_list[11], 71), 0)
    z_gate = draw_z_gate(jax.random.fold_in(key_list[11], 71), 0)
    conv_x = gaussian(key_list[4], (CONV, INNER), 0.5, 2.0, ((1, 4),), jnp.float32)
    conv_bc = gaussian(key_list[5], (2, CONV, GROUPS * STATE), 0.5, 2.0, ((2, 4),), jnp.float32)
    dt_bias = jnp.clip(jax.random.uniform(key_list[6], (HEADS,), jnp.float32, -0.3, 0.3) * steps_of(key_list[6], (HEADS,), ((0, 4),), -0.4, 0.0), -0.3, 0.3)
    a_log = draw_a_log(jax.random.fold_in(key_list[11], 71), 0)
    d_skip = jnp.clip(0.5 + 1.0 * jax.random.uniform(key_list[8], (HEADS,), jnp.float32) ** steps_of(key_list[8], (HEADS,), ((0, 4),), -0.2, 0.2), 0.5, 1.5)
    init_state = gaussian(key_list[9], (HEADS, HDIM, STATE), 1.0, 5.0, ((0, 4),), jnp.float32)
    norm_gain = jnp.clip(1.0 + 0.1 * jax.random.normal(key_list[10], (INNER,), jnp.float32), 0.5, 1.5)
    return {"x_input": x_input, "bc_input": bc_input, "dt_input": dt_input, "z_gate": z_gate, "conv_x": conv_x, "conv_bc": conv_bc, "dt_bias": dt_bias, "a_log": a_log, "d_skip": d_skip, "init_state": init_state, "norm_gain": norm_gain}


norm_eps = 1e-05

def reference(x_input, bc_input, dt_input, z_gate, conv_x, conv_bc, dt_bias, a_log, d_skip, init_state, norm_gain):
    group_heads = HEADS // GROUPS
    decay_rates = jnp.exp(a_log)
    x_padded = jnp.pad(x_input, ((CONV - 1, 0), (0, 0)))
    bc_padded = jnp.pad(bc_input, ((0, 0), (CONV - 1, 0), (0, 0)))
    causal = jnp.arange(SPAN)[:, None] >= jnp.arange(SPAN)[None, :]

    def advance(carry_state, token_position):
        row_start = (token_position * SPAN).astype(jnp.int32)
        x_rows = lax.dynamic_slice_in_dim(x_padded, row_start, SPAN + CONV - 1, 0)
        bc_rows = lax.dynamic_slice_in_dim(bc_padded, row_start, SPAN + CONV - 1, 1)
        x_sum = jnp.zeros((SPAN, INNER), jnp.float32)
        bc_sum = jnp.zeros((2, SPAN, GROUPS * STATE), jnp.float32)
        for tap_index in range(CONV):
            x_sum = x_sum + conv_x[tap_index] * x_rows[tap_index:tap_index + SPAN].astype(jnp.float32)
            bc_sum = bc_sum + conv_bc[:, tap_index][:, None, :] * bc_rows[:, tap_index:tap_index + SPAN].astype(jnp.float32)
        x_conv = jax.nn.silu(x_sum).astype(jnp.bfloat16)
        bc_conv = jax.nn.silu(bc_sum).astype(jnp.bfloat16)
        b_mat = bc_conv[0].reshape(SPAN, GROUPS, STATE).astype(jnp.float32)
        c_mat = bc_conv[1].reshape(SPAN, GROUPS, STATE).astype(jnp.float32)
        dt_rows = lax.dynamic_slice_in_dim(dt_input, row_start, SPAN, 0).astype(jnp.float32)
        time_step = jax.nn.softplus(dt_rows + dt_bias)
        log_cum = jnp.cumsum(-decay_rates * time_step, axis=0)
        scores = jnp.einsum('lgn,sgn->gls', c_mat, b_mat)
        cum_heads = log_cum.T
        log_gap = cum_heads[:, :, None] - cum_heads[:, None, :]
        weights = jnp.where(causal, jnp.exp(jnp.where(causal, log_gap, 0.0)), 0.0) * time_step.T[:, None, :]
        mixing = (scores[:, None] * weights.reshape(GROUPS, group_heads, SPAN, SPAN)).astype(jnp.bfloat16)
        x_heads = x_conv.reshape(SPAN, GROUPS, group_heads, HDIM).astype(jnp.float32)
        local_part = jnp.einsum('ghls,sghp->lghp', mixing.astype(jnp.float32), x_heads)
        grouped_state = carry_state.reshape(GROUPS, group_heads, HDIM, STATE)
        state_low = grouped_state.astype(jnp.bfloat16).astype(jnp.float32)
        carried_part = jnp.exp(log_cum).reshape(SPAN, GROUPS, group_heads, 1) * jnp.einsum('lgn,ghpn->lghp', c_mat, state_low, precision=lax.Precision.HIGHEST)
        skip_part = d_skip.reshape(GROUPS, group_heads, 1) * x_heads
        mixed_out = (local_part + carried_part + skip_part).reshape(SPAN, INNER)
        z_rows = lax.dynamic_slice_in_dim(z_gate, row_start, SPAN, 0).astype(jnp.float32)
        gated_out = mixed_out * jax.nn.silu(z_rows)
        mean_square = lax.optimization_barrier(jnp.mean(gated_out * gated_out, axis=1, keepdims=True))
        normed = (gated_out * lax.rsqrt(mean_square + norm_eps) * norm_gain).astype(jnp.bfloat16)
        tail_weight = jnp.exp(log_cum[-1:] - log_cum) * time_step
        x_weighted = (x_heads * tail_weight.reshape(SPAN, GROUPS, group_heads, 1)).astype(jnp.bfloat16)
        block_state = jnp.einsum('lghp,lgn->ghpn', x_weighted.astype(jnp.float32), b_mat)
        next_state = jnp.exp(log_cum[-1]).reshape(GROUPS, group_heads, 1, 1) * grouped_state + block_state
        return (next_state.reshape(HEADS, HDIM, STATE), normed)
    _, outputs = lax.scan(advance, init_state.astype(jnp.float32), jnp.arange(WINDOW_TOKENS // SPAN, dtype=jnp.int32))
    return outputs.reshape(WINDOW_TOKENS, INNER)
```

```python
import functools

import jax
import jax.numpy as jnp
from jax import lax
from jax.experimental import pallas as pl
from jax.experimental.pallas import tpu as pltpu
from jax.sharding import PartitionSpec as P

SPAN = 256
STEP_HEADS = 4
LANES = 128
LOG2E = 1.4426950408889634
norm_eps = 1e-05
VMEM = 56 * 1024 * 1024
f32 = jnp.float32
bf16 = jnp.bfloat16


def dot(a, b):
    return jnp.dot(a, b, preferred_element_type=f32)


def half_silu(h):
    return h + h * jnp.tanh(h)


def conv_half(halo, block, taps):
    full = jnp.concatenate([halo, block], axis=0)
    acc = block * taps[3:4]
    for back in range(1, 4):
        acc = acc + pltpu.roll(full, back, 0)[8:] * taps[3 - back : 4 - back]
    return acc


def prepare_kernel(dt_ref, bias_ref, alog_ref, bc_ref, rim_ref, taps_ref,
                   cols_ref, vrow_ref, dec_ref, c_ref, bt_ref):
    rows = dt_ref.shape[0]
    segments = rows // SPAN
    r = lax.broadcasted_iota(jnp.int32, (SPAN, SPAN), 0)
    c = lax.broadcasted_iota(jnp.int32, (SPAN, SPAN), 1)
    tri = (r >= c).astype(f32)
    lane = lax.broadcasted_iota(jnp.int32, (SPAN, LANES), 1) // (LANES // 4)
    rate = -jnp.exp(alog_ref[...]) * LOG2E
    pre = jnp.zeros((1, LANES), f32)
    decays = []
    for k in range(segments):
        at = slice(k * SPAN, (k + 1) * SPAN)
        v = dt_ref[at].astype(f32) + bias_ref[...]
        ts = jnp.maximum(v, 0.0) + jnp.log1p(jnp.exp(-jnp.abs(v)))
        cum = jnp.dot(tri, ts * rate, precision=lax.Precision.HIGHEST,
                      preferred_element_type=f32)
        end = cum[SPAN - 1 : SPAN]
        vrow_ref[:, at] = (cum - jnp.log2(ts)).T[: LANES // 4]
        tail = jnp.exp2(end - cum) * ts
        cols_ref[at] = jnp.where(
            lane == 0, cum,
            jnp.where(lane == 1, jnp.exp2(cum),
                      jnp.where(lane == 2, tail, jnp.exp2(cum + pre))))
        decays.append(jnp.exp2(end))
        pre = pre + end
    decays.append(jnp.exp2(pre))
    decays.append(jnp.zeros((8 - len(decays), LANES), f32))
    dec_ref[...] = jnp.concatenate(decays, axis=0)
    for i in range(2):
        taps = taps_ref[i] * 0.5
        halo = rim_ref[i]
        for k in range(segments):
            at = slice(k * SPAN, (k + 1) * SPAN)
            block = bc_ref[i, at].astype(f32)
            out = half_silu(conv_half(halo, block, taps))
            halo = block[SPAN - 8 :]
            if i == 0:
                bt_ref[:, at] = out.T.astype(bf16)
            else:
                c_ref[at] = out.astype(bf16)


def turned(ref_value, width=LANES):
    step = pl.program_id(0)
    return pltpu.roll(ref_value, lax.rem(LANES - step * STEP_HEADS, LANES), 1)


def states_kernel(x_ref, rim_ref, taps_ref, cols_ref, dec_ref, bt_ref,
                  xc_ref, starts_ref, sum_ref, halo_ref, turn_ref):
    rows = x_ref.shape[0]
    segments = rows // SPAN
    turn_ref[...] = turned(cols_ref[...])
    dec = turned(dec_ref[...])
    halo_ref[...] = rim_ref[...]
    running = None
    for k in range(segments):
        at = slice(k * SPAN, (k + 1) * SPAN)
        weighted = []
        for j in range(STEP_HEADS):
            lanes = slice(j * LANES, (j + 1) * LANES)
            block = x_ref[at, lanes].astype(f32)
            if k == 0:
                halo = halo_ref[:, lanes]
            else:
                halo = x_ref[k * SPAN - 16 : k * SPAN, lanes].astype(f32)[8:]
            xc = half_silu(conv_half(halo, block, taps_ref[:, lanes] * 0.5)).astype(bf16)
            xc_ref[at, lanes] = xc
            tail = turn_ref[at, 64 + j : 65 + j]
            weighted.append((xc.astype(f32) * tail).astype(bf16))
        fresh = dot(bt_ref[:, at], jnp.concatenate(weighted, axis=1))
        nxt = []
        for j in range(STEP_HEADS):
            piece = fresh[:, j * LANES : (j + 1) * LANES]
            if k > 0:
                starts_ref[k - 1, :, j * LANES : (j + 1) * LANES] = running[j].astype(bf16)
                piece = piece + dec[k : k + 1, j : j + 1] * running[j]
            nxt.append(piece)
        running = nxt
    for j in range(STEP_HEADS):
        sum_ref[j] = running[j].astype(sum_ref.dtype)


def local_kernel(xc_ref, cols_ref, vrow_ref, c_ref, bt_ref, starts_ref, skip_ref,
                 out_ref, turn_ref):
    rows = xc_ref.shape[0]
    segments = rows // SPAN
    half = SPAN // 2
    turn_ref[...] = turned(cols_ref[...])
    r = lax.broadcasted_iota(jnp.int32, (half, half), 0)
    c = lax.broadcasted_iota(jnp.int32, (half, half), 1)
    causal = r >= c
    for k in range(segments):
        base = k * SPAN
        at = slice(base, base + SPAN)
        top, low = slice(base, base + half), slice(base + half, base + SPAN)
        scores = dot(c_ref[at], bt_ref[:, at])
        s_tt = jnp.where(causal, scores[:half, :half], 0.0)
        s_lt = scores[half:, :half]
        s_ll = jnp.where(causal, scores[half:, half:], 0.0)
        if k > 0:
            carried = dot(c_ref[at], starts_ref[k - 1])
        for j in range(STEP_HEADS):
            lanes = slice(j * LANES, (j + 1) * LANES)
            u = turn_ref[at, j : j + 1]
            v = vrow_ref[0, j : j + 1, at]
            m_tt = s_tt * jnp.exp2(jnp.minimum(u[:half] - v[:, :half], 100.0))
            m_lt = s_lt * jnp.exp2(u[half:] - v[:, :half])
            m_ll = s_ll * jnp.exp2(jnp.minimum(u[half:] - v[:, half:], 100.0))
            x = xc_ref[at, lanes]
            y_t = dot(m_tt.astype(bf16), x[:half])
            y_l = dot(jnp.concatenate([m_lt, m_ll], axis=1).astype(bf16), x)
            y = jnp.concatenate([y_t, y_l], axis=0) + skip_ref[:, lanes] * x.astype(f32)
            if k > 0:
                y = y + turn_ref[at, 32 + j : 33 + j] * carried[:, lanes]
            out_ref[at, lanes] = y


def gate_kernel(part_ref, z_ref, cols_ref, c_ref, inc_ref, out_ref, sq_ref):
    cols = turned(cols_ref[...])
    rows = part_ref.shape[0]

    @pl.when(pl.program_id(0) == 0)
    def _():
        sq_ref[...] = jnp.zeros_like(sq_ref)

    for k in range(rows // SPAN):
        at = slice(k * SPAN, (k + 1) * SPAN)
        total = sq_ref[at]
        for j in range(STEP_HEADS):
            lanes = slice(j * LANES, (j + 1) * LANES)
            carried = dot(c_ref[at], inc_ref[j])
            mixed = part_ref[at, lanes] + cols[at, 96 + j : 97 + j] * carried
            gated = mixed * half_silu(z_ref[at, lanes].astype(f32) * 0.5)
            total = total + gated * gated
            out_ref[at, lanes] = gated.astype(out_ref.dtype)
        sq_ref[at] = total


def local(x_input, bc_input, dt_input, z_gate, conv_x, conv_bc, dt_bias, a_log,
          d_skip, init_state, norm_gain, *, inner):
    rows, channels = x_input.shape
    heads = a_log.shape[0]
    state = init_state.shape[2]
    groups = bc_input.shape[2] // state
    steps = heads // STEP_HEADS
    per_group = steps // groups
    width = STEP_HEADS * LANES
    segments = rows // SPAN
    n = lax.axis_size("seq")
    me = lax.axis_index("seq")
    group_cols = bc_input.shape[2]

    tail = jnp.concatenate(
        [x_input[rows - 8 :], bc_input[0, rows - 8 :], bc_input[1, rows - 8 :]], axis=1)
    rim = lax.ppermute(tail, "seq", [(i, i + 1) for i in range(n - 1)]).astype(f32)
    x_rim = rim[:, :channels]
    bc_rim = jnp.stack([rim[:, channels : channels + group_cols], rim[:, channels + group_cols :]])

    params = functools.partial(pltpu.CompilerParams, vmem_limit_bytes=VMEM)
    four = lambda a: jnp.concatenate([a] * 4, axis=-1)
    cols, vrow, dec, c_mat, b_t = pl.pallas_call(
        prepare_kernel,
        out_shape=(
            jax.ShapeDtypeStruct((rows, LANES), f32),
            jax.ShapeDtypeStruct((heads, rows), f32),
            jax.ShapeDtypeStruct((8, LANES), f32),
            jax.ShapeDtypeStruct((rows, group_cols), bf16),
            jax.ShapeDtypeStruct((group_cols, rows), bf16),
        ),
        compiler_params=params(),
        name="prepare",
    )(four(dt_input), four(dt_bias)[None], four(a_log)[None], bc_input, bc_rim, conv_bc)
    vrow = vrow.reshape(steps, STEP_HEADS, rows)

    whole = lambda shape: pl.BlockSpec(shape, lambda i: (0,) * len(shape))
    stripe = pl.BlockSpec((rows, width), lambda i: (0, i))
    bt_spec = pl.BlockSpec((state, rows), lambda i: (i // per_group, 0))
    c_spec = pl.BlockSpec((rows, state), lambda i: (0, i // per_group))
    cols_spec = whole((rows, LANES))
    starts_spec = pl.BlockSpec((segments - 1, state, width), lambda i: (0, 0, i))
    heads_spec = pl.BlockSpec((STEP_HEADS, state, LANES), lambda i: (i, 0, 0))
    x_conv, starts, summary = pl.pallas_call(
        states_kernel,
        grid=(steps,),
        in_specs=[stripe, pl.BlockSpec((8, width), lambda i: (0, i)),
                  pl.BlockSpec((4, width), lambda i: (0, i)), cols_spec, whole((8, LANES)), bt_spec],
        out_specs=(stripe, starts_spec, heads_spec),
        out_shape=(
            jax.ShapeDtypeStruct((rows, channels), bf16),
            jax.ShapeDtypeStruct((segments - 1, state, channels), bf16),
            jax.ShapeDtypeStruct((heads, state, LANES), bf16),
        ),
        scratch_shapes=[pltpu.VMEM((8, width), f32), pltpu.VMEM((rows, LANES), f32)],
        compiler_params=params(),
        name="states",
    )(x_input, x_rim, conv_x, cols, dec, b_t)

    partial = pl.pallas_call(
        local_kernel,
        grid=(steps,),
        in_specs=[stripe, cols_spec, pl.BlockSpec((1, STEP_HEADS, rows), lambda i: (i, 0, 0)),
                  c_spec, bt_spec, starts_spec, pl.BlockSpec((1, width), lambda i: (0, i))],
        out_specs=stripe,
        out_shape=jax.ShapeDtypeStruct((rows, channels), f32),
        scratch_shapes=[pltpu.VMEM((rows, LANES), f32)],
        compiler_params=params(),
        cost_estimate=pl.CostEstimate(flops=8 * 10**9, bytes_accessed=40 * 2**20, transcendentals=0),
        name="inside",
    )(x_conv, cols, vrow, c_mat, b_t, starts, jnp.repeat(d_skip, LANES)[None])

    factor = lax.all_gather(dec[segments, :heads], "seq", axis=0)
    share = heads // n
    got = lax.all_to_all(summary, "seq", split_axis=0, concat_axis=0, tiled=True)
    got = got.reshape(n, share, state, LANES).astype(f32)
    mine = lax.dynamic_slice_in_dim(factor, me * share, share, 1)[:, :, None, None]
    seed = lax.dynamic_slice_in_dim(init_state, me * share, share, 0).transpose(0, 2, 1)
    running = seed
    sent = []
    for i in range(n):
        sent.append(running.astype(bf16))
        running = mine[i] * running + got[i]
    incoming = lax.all_to_all(jnp.concatenate(sent, axis=0), "seq", split_axis=0, concat_axis=0,
                              tiled=True)

    gated, squares = pl.pallas_call(
        gate_kernel,
        grid=(steps,),
        in_specs=[stripe, stripe, cols_spec, c_spec, heads_spec],
        out_specs=(stripe, cols_spec),
        out_shape=(jax.ShapeDtypeStruct((rows, channels), f32),
                   jax.ShapeDtypeStruct((rows, LANES), f32)),
        compiler_params=params(),
        name="gate",
    )(partial, z_gate, cols, c_mat, incoming)
    total = lax.psum(jnp.sum(squares, axis=1), "head")
    inverse = lax.rsqrt(total / inner + norm_eps)
    return (gated * inverse[:, None] * norm_gain).astype(bf16)


def solution(mesh):
    placed = (
        P("seq", "head"), P(None, "seq", "head"), P("seq", "head"), P("seq", "head"),
        P(None, "head"), P(None, None, "head"), P("head"), P("head"), P("head"),
        P("head", None, None), P("head"),
    )

    def run(*args):
        return jax.shard_map(
            functools.partial(local, inner=args[0].shape[1]),
            mesh=mesh, in_specs=placed, out_specs=P("seq", "head"), check_vma=False,
        )(*args)

    return run
```

```python
import functools

import jax
import jax.numpy as jnp
from jax import lax
from jax.experimental import pallas as pl
from jax.experimental.pallas import tpu as pltpu
from jax.sharding import PartitionSpec as P

SPAN = 256
STEP_HEADS = 4
LANES = 128
LOG2E = 1.4426950408889634
RELAY_FROM = 2
norm_eps = 1e-05
VMEM = 56 * 1024 * 1024
f32 = jnp.float32
bf16 = jnp.bfloat16


def dot(a, b):
    return jnp.dot(a, b, preferred_element_type=f32)


def half_silu(h):
    return h + h * jnp.tanh(h)


def conv_half(halo, block, taps):
    full = jnp.concatenate([halo, block], axis=0)
    acc = block * taps[3:4]
    for back in range(1, 4):
        acc = acc + pltpu.roll(full, back, 0)[8:] * taps[3 - back : 4 - back]
    return acc


def prepare_kernel(dt_ref, bias_ref, alog_ref, bc_ref, rim_ref, taps_ref,
                   cols_ref, vrow_ref, dec_ref, c_ref, bt_ref):
    rows = dt_ref.shape[0]
    segments = rows // SPAN
    r = lax.broadcasted_iota(jnp.int32, (SPAN, SPAN), 0)
    c = lax.broadcasted_iota(jnp.int32, (SPAN, SPAN), 1)
    tri = (r >= c).astype(f32)
    lane = lax.broadcasted_iota(jnp.int32, (SPAN, LANES), 1) // (LANES // 4)
    rate = -jnp.exp(alog_ref[...]) * LOG2E
    pre = jnp.zeros((1, LANES), f32)
    decays = []
    for k in range(segments):
        at = slice(k * SPAN, (k + 1) * SPAN)
        v = dt_ref[at].astype(f32) + bias_ref[...]
        ts = jnp.maximum(v, 0.0) + jnp.log1p(jnp.exp(-jnp.abs(v)))
        cum = jnp.dot(tri, ts * rate, precision=lax.Precision.HIGHEST,
                      preferred_element_type=f32)
        end = cum[SPAN - 1 : SPAN]
        vrow_ref[:, at] = (cum - jnp.log2(ts)).T[: LANES // 4]
        tail = jnp.exp2(end - cum) * ts
        cols_ref[at] = jnp.where(
            lane == 0, cum,
            jnp.where(lane == 1, jnp.exp2(cum),
                      jnp.where(lane == 2, tail, jnp.exp2(cum + pre))))
        decays.append(jnp.exp2(end))
        pre = pre + end
    decays.append(jnp.exp2(pre))
    decays.append(jnp.zeros((8 - len(decays), LANES), f32))
    dec_ref[...] = jnp.concatenate(decays, axis=0)
    for i in range(2):
        taps = taps_ref[i] * 0.5
        halo = rim_ref[i]
        for k in range(segments):
            at = slice(k * SPAN, (k + 1) * SPAN)
            block = bc_ref[i, at].astype(f32)
            out = half_silu(conv_half(halo, block, taps))
            halo = block[SPAN - 8 :]
            if i == 0:
                bt_ref[:, at] = out.T.astype(bf16)
            else:
                c_ref[at] = out.astype(bf16)


def turned(ref_value, width=LANES):
    step = pl.program_id(0)
    return pltpu.roll(ref_value, lax.rem(LANES - step * STEP_HEADS, LANES), 1)


def states_kernel(x_ref, rim_ref, taps_ref, cols_ref, dec_ref, bt_ref,
                  xc_ref, starts_ref, sum_ref, fade_ref, halo_ref, turn_ref):
    rows = x_ref.shape[0]
    segments = rows // SPAN
    turn_ref[...] = turned(cols_ref[...])
    dec = turned(dec_ref[...])
    halo_ref[...] = rim_ref[...]
    running = None
    for k in range(segments):
        at = slice(k * SPAN, (k + 1) * SPAN)
        weighted = []
        for j in range(STEP_HEADS):
            lanes = slice(j * LANES, (j + 1) * LANES)
            block = x_ref[at, lanes].astype(f32)
            if k == 0:
                halo = halo_ref[:, lanes]
            else:
                halo = x_ref[k * SPAN - 16 : k * SPAN, lanes].astype(f32)[8:]
            xc = half_silu(conv_half(halo, block, taps_ref[:, lanes] * 0.5)).astype(bf16)
            xc_ref[at, lanes] = xc
            tail = turn_ref[at, 64 + j : 65 + j]
            weighted.append((xc.astype(f32) * tail).astype(bf16))
        fresh = dot(bt_ref[:, at], jnp.concatenate(weighted, axis=1))
        nxt = []
        for j in range(STEP_HEADS):
            piece = fresh[:, j * LANES : (j + 1) * LANES]
            if k > 0:
                starts_ref[k - 1, :, j * LANES : (j + 1) * LANES] = running[j].astype(bf16)
                piece = piece + dec[k : k + 1, j : j + 1] * running[j]
            nxt.append(piece)
        running = nxt
    for j in range(STEP_HEADS):
        sum_ref[j] = running[j].astype(sum_ref.dtype)
        fade_ref[j] = jnp.broadcast_to(dec[segments : segments + 1, j : j + 1], (8, LANES))


def inside(xc_ref, turn_ref, vrow_ref, c_ref, bt_ref, starts_ref, skip_ref, out_ref):
    rows = xc_ref.shape[0]
    segments = rows // SPAN
    half = SPAN // 2
    r = lax.broadcasted_iota(jnp.int32, (half, half), 0)
    c = lax.broadcasted_iota(jnp.int32, (half, half), 1)
    causal = r >= c
    for k in range(segments):
        base = k * SPAN
        at = slice(base, base + SPAN)
        scores = dot(c_ref[at], bt_ref[:, at])
        s_tt = jnp.where(causal, scores[:half, :half], 0.0)
        s_lt = scores[half:, :half]
        s_ll = jnp.where(causal, scores[half:, half:], 0.0)
        if k > 0:
            carried = dot(c_ref[at], starts_ref[k - 1])
        for j in range(STEP_HEADS):
            lanes = slice(j * LANES, (j + 1) * LANES)
            u = turn_ref[at, j : j + 1]
            v = vrow_ref[0, j : j + 1, at]
            m_tt = s_tt * jnp.exp2(jnp.minimum(u[:half] - v[:, :half], 100.0))
            m_lt = s_lt * jnp.exp2(u[half:] - v[:, :half])
            m_ll = s_ll * jnp.exp2(jnp.minimum(u[half:] - v[:, half:], 100.0))
            x = xc_ref[at, lanes]
            y_t = dot(m_tt.astype(bf16), x[:half])
            y_l = dot(jnp.concatenate([m_lt, m_ll], axis=1).astype(bf16), x)
            y = jnp.concatenate([y_t, y_l], axis=0) + skip_ref[:, lanes] * x.astype(f32)
            if k > 0:
                y = y + turn_ref[at, 32 + j : 33 + j] * carried[:, lanes]
            out_ref[at, lanes] = y


def gate(part_ref, z_ref, turn_ref, c_ref, inc_ref, out_ref, sq_ref):
    rows = part_ref.shape[0]
    for k in range(rows // SPAN):
        at = slice(k * SPAN, (k + 1) * SPAN)
        total = sq_ref[at]
        for j in range(STEP_HEADS):
            lanes = slice(j * LANES, (j + 1) * LANES)
            carried = dot(c_ref[at], inc_ref[j])
            mixed = part_ref[at, lanes] + turn_ref[at, 96 + j : 97 + j] * carried
            gated = mixed * half_silu(z_ref[at, lanes].astype(f32) * 0.5)
            total = total + gated * gated
            out_ref[at, lanes] = gated
        sq_ref[at] = total


def mix_kernel(steps, peers, pairs, inner,
               xc_ref, z_ref, cols_ref, vrow_ref, c_ref, bt_ref, starts_ref, skip_ref,
               sum_ref, fade_ref, init_ref,
               out_ref, inv_ref,
               part_ref, turn_ref, sq_ref, near_ref, near_fade_ref, back_ref, ahead_ref,
               give_ref, inc_ref, now_ref, rows_ref, got_ref,
               near_send, near_recv, fade_send, fade_recv, chain_send, chain_recv,
               give_send, give_recv, sq_send, sq_recv):
    i = pl.program_id(0)
    me = lax.axis_index("seq")
    mine = lax.axis_index("head")
    side = lax.rem(me, 2)
    pair = me // 2
    partner = me + 1 - 2 * side
    chunks = steps // 2
    own = side * chunks
    other = chunks - own

    def to_seq(src, dst, send, recv, target):
        return pltpu.make_async_remote_copy(
            src_ref=src, dst_ref=dst, send_sem=send, recv_sem=recv,
            device_id={"seq": target}, device_id_type=pl.DeviceIdType.MESH)

    def near(c):
        return to_seq(sum_ref.at[pl.ds((other + c) * STEP_HEADS, STEP_HEADS)], near_ref.at[c],
                      near_send.at[c], near_recv.at[c], partner)

    def near_fade():
        return to_seq(fade_ref.at[pl.ds(other * STEP_HEADS, chunks * STEP_HEADS)], near_fade_ref,
                      fade_send, fade_recv, partner)

    def chain(c, target):
        return to_seq(ahead_ref.at[c], back_ref.at[c], chain_send.at[c], chain_recv.at[c], target)

    def give(c):
        return to_seq(give_ref.at[c], inc_ref.at[own + c], give_send.at[c], give_recv.at[c], partner)

    def squares(p):
        return pltpu.make_async_remote_copy(
            src_ref=rows_ref, dst_ref=got_ref.at[p - 1], send_sem=sq_send.at[p - 1],
            recv_sem=sq_recv.at[p - 1], device_id={"head": lax.rem(mine + p, peers)},
            device_id_type=pl.DeviceIdType.MESH)

    @pl.when(i == 0)
    def _():
        barrier = pltpu.get_barrier_semaphore()

        def greet(**where):
            pl.semaphore_signal(barrier, inc=1, device_id=where,
                                device_id_type=pl.DeviceIdType.MESH)

        greet(seq=partner)
        for p in range(1, peers):
            greet(head=lax.rem(mine + p, peers))

        @pl.when(pair > 0)
        def _():
            greet(seq=me - 2)

        @pl.when(pair < pairs - 1)
        def _():
            greet(seq=me + 2)

        pl.semaphore_wait(
            barrier, peers + jnp.minimum(pair, 1) + jnp.minimum(pairs - 1 - pair, 1))
        near_fade().start()
        for c in range(chunks):
            near(c).start()
        sq_ref[...] = jnp.zeros_like(sq_ref)

    def relay(c):
        if c == 0:
            near_fade().wait_recv()
        near(c).wait_recv()

        @pl.when(pair == 0)
        def _():
            for j in range(STEP_HEADS):
                now_ref[j] = init_ref[(own + c) * STEP_HEADS + j].T

        @pl.when(pair > 0)
        def _():
            chain(c, partner).wait_recv()
            now_ref[...] = back_ref[c].astype(f32)

        for j in range(STEP_HEADS):
            h = (own + c) * STEP_HEADS + j
            here, there = sum_ref[h].astype(f32), near_ref[c, j].astype(f32)
            d_here = fade_ref[h][0:1]
            d_there = near_fade_ref[c * STEP_HEADS + j][0:1]
            even = side == 0
            first = now_ref[j]
            second = (jnp.where(even, d_here, d_there) * first
                      + jnp.where(even, here, there))
            last = (jnp.where(even, d_there, d_here) * second
                    + jnp.where(even, there, here))
            inc_ref[own + c, j] = jnp.where(even, first, second).astype(bf16)
            give_ref[c, j] = jnp.where(even, second, first).astype(bf16)
            ahead_ref[c, j] = last.astype(bf16)

        @pl.when(pair < pairs - 1)
        def _():
            chain(c, me + 2).start()

        give(c).start()

    for c in range(chunks):
        pl.when(i == jnp.minimum(RELAY_FROM + c + pair, steps))(functools.partial(relay, c))

    step = lax.rem(i, steps)
    turn_ref[...] = pltpu.roll(cols_ref[...], lax.rem(LANES - step * STEP_HEADS, LANES), 1)

    @pl.when(i < steps)
    def _():
        inside(xc_ref, turn_ref, vrow_ref, c_ref, bt_ref, starts_ref, skip_ref, part_ref.at[step])

    @pl.when(i >= steps)
    def _():
        for c in range(chunks):
            pl.when(step == other + c)(lambda c=c: give(c).wait_recv())
        gate(part_ref.at[step], z_ref, turn_ref, c_ref, inc_ref.at[step], out_ref, sq_ref)

    @pl.when(i == 2 * steps - 1)
    def _():
        count = rows_ref.shape[0]
        for q in range(count):
            rows_ref[q : q + 1] = jnp.sum(sq_ref[q * LANES : (q + 1) * LANES].T, axis=0,
                                          keepdims=True)
        for p in range(1, peers):
            squares(p).start()
        near_fade().wait_send()
        for c in range(chunks):
            near(c).wait_send()
            give(c).wait_send()

        @pl.when(pair < pairs - 1)
        def _():
            for c in range(chunks):
                chain(c, partner).wait_send()

        total = rows_ref[...]
        for p in range(1, peers):
            squares(p).wait_recv()
            total = total + got_ref[p - 1]
        inv_ref[...] = lax.rsqrt(total / inner + norm_eps)
        for p in range(1, peers):
            squares(p).wait_send()


def local(x_input, bc_input, dt_input, z_gate, conv_x, conv_bc, dt_bias, a_log,
          d_skip, init_state, norm_gain, *, inner):
    rows, channels = x_input.shape
    heads = a_log.shape[0]
    state = init_state.shape[2]
    groups = bc_input.shape[2] // state
    steps = heads // STEP_HEADS
    per_group = steps // groups
    width = STEP_HEADS * LANES
    segments = rows // SPAN
    n = lax.axis_size("seq")
    group_cols = bc_input.shape[2]

    tail = jnp.concatenate(
        [x_input[rows - 8 :], bc_input[0, rows - 8 :], bc_input[1, rows - 8 :]], axis=1)
    rim = lax.ppermute(tail, "seq", [(i, i + 1) for i in range(n - 1)]).astype(f32)
    x_rim = rim[:, :channels]
    bc_rim = jnp.stack([rim[:, channels : channels + group_cols], rim[:, channels + group_cols :]])

    params = functools.partial(pltpu.CompilerParams, vmem_limit_bytes=VMEM)
    four = lambda a: jnp.concatenate([a] * 4, axis=-1)
    cols, vrow, dec, c_mat, b_t = pl.pallas_call(
        prepare_kernel,
        out_shape=(
            jax.ShapeDtypeStruct((rows, LANES), f32),
            jax.ShapeDtypeStruct((heads, rows), f32),
            jax.ShapeDtypeStruct((8, LANES), f32),
            jax.ShapeDtypeStruct((rows, group_cols), bf16),
            jax.ShapeDtypeStruct((group_cols, rows), bf16),
        ),
        compiler_params=params(),
        name="prepare",
    )(four(dt_input), four(dt_bias)[None], four(a_log)[None], bc_input, bc_rim, conv_bc)
    vrow = vrow.reshape(steps, STEP_HEADS, rows)

    whole = lambda shape: pl.BlockSpec(shape, lambda i: (0,) * len(shape))
    stripe = pl.BlockSpec((rows, width), lambda i: (0, i))
    bt_spec = pl.BlockSpec((state, rows), lambda i: (i // per_group, 0))
    cols_spec = whole((rows, LANES))
    starts_spec = pl.BlockSpec((segments - 1, state, width), lambda i: (0, 0, i))
    heads_spec = pl.BlockSpec((STEP_HEADS, state, LANES), lambda i: (i, 0, 0))
    x_conv, starts, summary, fade = pl.pallas_call(
        states_kernel,
        grid=(steps,),
        in_specs=[stripe, pl.BlockSpec((8, width), lambda i: (0, i)),
                  pl.BlockSpec((4, width), lambda i: (0, i)), cols_spec, whole((8, LANES)), bt_spec],
        out_specs=(stripe, starts_spec, heads_spec,
                   pl.BlockSpec((STEP_HEADS, 8, LANES), lambda i: (i, 0, 0))),
        out_shape=(
            jax.ShapeDtypeStruct((rows, channels), bf16),
            jax.ShapeDtypeStruct((segments - 1, state, channels), bf16),
            jax.ShapeDtypeStruct((heads, state, LANES), bf16),
            jax.ShapeDtypeStruct((heads, 8, LANES), f32),
        ),
        scratch_shapes=[pltpu.VMEM((8, width), f32), pltpu.VMEM((rows, LANES), f32)],
        compiler_params=params(),
        name="states",
    )(x_input, x_rim, conv_x, cols, dec, b_t)

    chunks = steps // 2
    some = (chunks, STEP_HEADS, state, LANES)
    peers = lax.axis_size("head")
    now = lambda i: lax.rem(i, steps)
    soon = lambda i: jnp.minimum(i, steps - 1)
    late = lambda i: jnp.maximum(i - steps, 0)
    dma = pltpu.SemaphoreType.DMA
    gated, inverse = pl.pallas_call(
        functools.partial(mix_kernel, steps, peers, n // 2, inner),
        grid=(2 * steps,),
        in_specs=[
            pl.BlockSpec((rows, width), lambda i: (0, soon(i))),
            pl.BlockSpec((rows, width), lambda i: (0, late(i))),
            cols_spec,
            pl.BlockSpec((1, STEP_HEADS, rows), lambda i: (soon(i), 0, 0)),
            pl.BlockSpec((rows, state), lambda i: (0, now(i) // per_group)),
            pl.BlockSpec((state, rows), lambda i: (soon(i) // per_group, 0)),
            pl.BlockSpec((segments - 1, state, width), lambda i: (0, 0, soon(i))),
            pl.BlockSpec((1, width), lambda i: (0, soon(i))),
            whole((heads, state, LANES)),
            whole((heads, 8, LANES)),
            whole((heads, LANES, state)),
        ],
        out_specs=(pl.BlockSpec((rows, width), lambda i: (0, late(i))),
                   whole((rows // LANES, LANES))),
        out_shape=(jax.ShapeDtypeStruct((rows, channels), f32),
                   jax.ShapeDtypeStruct((rows // LANES, LANES), f32)),
        scratch_shapes=[
            pltpu.VMEM((steps, rows, width), f32),
            pltpu.VMEM((rows, LANES), f32),
            pltpu.VMEM((rows, LANES), f32),
            pltpu.VMEM(some, bf16),
            pltpu.VMEM((heads // 2, 8, LANES), f32),
            pltpu.VMEM(some, bf16),
            pltpu.VMEM(some, bf16),
            pltpu.VMEM(some, bf16),
            pltpu.VMEM((steps, STEP_HEADS, state, LANES), bf16),
            pltpu.VMEM((STEP_HEADS, state, LANES), f32),
            pltpu.VMEM((rows // LANES, LANES), f32),
            pltpu.VMEM((peers - 1, rows // LANES, LANES), f32),
            dma((chunks,)), dma((chunks,)), dma, dma, dma((chunks,)), dma((chunks,)),
            dma((chunks,)), dma((chunks,)), dma((peers - 1,)), dma((peers - 1,)),
        ],
        compiler_params=params(collective_id=0, has_side_effects=True),
        cost_estimate=pl.CostEstimate(flops=8 * 10**9, bytes_accessed=40 * 2**20, transcendentals=0),
        name="mix",
    )(x_conv, z_gate, cols, vrow, c_mat, b_t, starts, jnp.repeat(d_skip, LANES)[None],
      summary, fade, init_state)
    return (gated * inverse.reshape(rows, 1) * norm_gain).astype(bf16)


def solution(mesh):
    placed = (
        P("seq", "head"), P(None, "seq", "head"), P("seq", "head"), P("seq", "head"),
        P(None, "head"), P(None, None, "head"), P("head"), P("head"), P("head"),
        P("head", None, None), P("head"),
    )

    def run(*args):
        return jax.shard_map(
            functools.partial(local, inner=args[0].shape[1]),
            mesh=mesh, in_specs=placed, out_specs=P("seq", "head"), check_vma=False,
        )(*args)

    return run
```

```python
import functools

import jax
import jax.numpy as jnp
from jax import lax
from jax.experimental import pallas as pl
from jax.experimental.pallas import tpu as pltpu
from jax.sharding import PartitionSpec as P

SPAN = 256
STEP_HEADS = 4
LANES = 128
LOG2E = 1.4426950408889634
RELAY_FROM = 2
RIM = 16
norm_eps = 1e-05
VMEM = 56 * 1024 * 1024
f32 = jnp.float32
bf16 = jnp.bfloat16


def dot(a, b):
    return jnp.dot(a, b, preferred_element_type=f32)


def half_silu(h):
    return h + h * jnp.tanh(h)


def conv_half(halo, block, taps):
    full = jnp.concatenate([halo, block], axis=0)
    acc = block * taps[3:4]
    for back in range(1, 4):
        acc = acc + pltpu.roll(full, back, 0)[8:] * taps[3 - back : 4 - back]
    return acc


def prepare_kernel(count, x_ref, dt_ref, bias_ref, alog_ref, bc_ref, taps_ref,
                   cols_ref, vrow_ref, dec_ref, c_ref, bt_ref, x_rim_ref,
                   x_got_ref, bc_got_ref, bc_rim_ref, x_send, x_recv, bc_send, bc_recv):
    rows = dt_ref.shape[0]
    segments = rows // SPAN
    heads_here = dt_ref.shape[1]
    me = lax.axis_index("seq")
    barrier = pltpu.get_barrier_semaphore()

    def to_next(src, dst, send, recv):
        return pltpu.make_async_remote_copy(
            src_ref=src, dst_ref=dst, send_sem=send, recv_sem=recv,
            device_id={"seq": jnp.minimum(me + 1, count - 1)},
            device_id_type=pl.DeviceIdType.MESH)

    x_copy = to_next(x_ref.at[pl.ds(rows - RIM, RIM)], x_got_ref, x_send, x_recv)
    bc_copy = to_next(bc_ref.at[:, pl.ds(rows - RIM, RIM)], bc_got_ref, bc_send, bc_recv)

    @pl.when(me > 0)
    def _():
        pl.semaphore_signal(barrier, inc=1, device_id={"seq": me - 1},
                            device_id_type=pl.DeviceIdType.MESH)

    @pl.when(me < count - 1)
    def _():
        pl.semaphore_signal(barrier, inc=1, device_id={"seq": me + 1},
                            device_id_type=pl.DeviceIdType.MESH)

    pl.semaphore_wait(barrier, jnp.minimum(me, 1) + jnp.minimum(count - 1 - me, 1))

    @pl.when(me < count - 1)
    def _():
        bc_copy.start()
        x_copy.start()

    rep = (lax.broadcasted_iota(jnp.int32, (heads_here, LANES), 0)
           == lax.broadcasted_iota(jnp.int32, (heads_here, LANES), 1) % heads_here)
    rep = rep.astype(f32)

    def spread(row):
        return jnp.dot(jnp.broadcast_to(row, (8, heads_here)), rep,
                       precision=lax.Precision.HIGHEST, preferred_element_type=f32)[:1]

    r = lax.broadcasted_iota(jnp.int32, (SPAN, SPAN), 0)
    c = lax.broadcasted_iota(jnp.int32, (SPAN, SPAN), 1)
    tri = (r >= c).astype(f32)
    lane = lax.broadcasted_iota(jnp.int32, (SPAN, LANES), 1) // (LANES // 4)
    rate = -jnp.exp(spread(alog_ref[...])) * LOG2E
    bias = spread(bias_ref[...])
    pre = jnp.zeros((1, LANES), f32)
    decays = []
    for k in range(segments):
        at = slice(k * SPAN, (k + 1) * SPAN)
        v = dot(dt_ref[at], rep.astype(bf16)) + bias
        ts = jnp.maximum(v, 0.0) + jnp.log1p(jnp.exp(-jnp.abs(v)))
        cum = jnp.dot(tri, ts * rate, precision=lax.Precision.HIGHEST,
                      preferred_element_type=f32)
        end = cum[SPAN - 1 : SPAN]
        v_rows = (cum - jnp.log2(ts)).T
        for g in range(heads_here // STEP_HEADS):
            vrow_ref[g, :, at] = v_rows[g * STEP_HEADS : (g + 1) * STEP_HEADS]
        tail = jnp.exp2(end - cum) * ts
        cols_ref[at] = jnp.where(
            lane == 0, cum,
            jnp.where(lane == 1, jnp.exp2(cum),
                      jnp.where(lane == 2, tail, jnp.exp2(cum + pre))))
        decays.append(jnp.exp2(end))
        pre = pre + end
    decays.append(jnp.exp2(pre))
    decays.append(jnp.zeros((8 - len(decays), LANES), f32))
    dec_ref[...] = jnp.concatenate(decays, axis=0)

    @pl.when(me > 0)
    def _():
        bc_copy.wait_recv()
        x_copy.wait_recv()
        bc_rim_ref[...] = bc_got_ref[...].astype(f32)
        x_rim_ref[...] = x_got_ref[...].astype(f32)

    @pl.when(me == 0)
    def _():
        bc_rim_ref[...] = jnp.zeros_like(bc_rim_ref)
        x_rim_ref[...] = jnp.zeros_like(x_rim_ref)

    for i in range(2):
        taps = taps_ref[i] * 0.5
        halo = bc_rim_ref[i, RIM - 8 :]
        for k in range(segments):
            at = slice(k * SPAN, (k + 1) * SPAN)
            block = bc_ref[i, at].astype(f32)
            out = half_silu(conv_half(halo, block, taps))
            halo = block[SPAN - 8 :]
            if i == 0:
                bt_ref[:, at] = out.T.astype(bf16)
            else:
                c_ref[at] = out.astype(bf16)

    @pl.when(me < count - 1)
    def _():
        bc_copy.wait_send()
        x_copy.wait_send()


def turned(ref_value, width=LANES):
    step = pl.program_id(0)
    return pltpu.roll(ref_value, lax.rem(LANES - step * STEP_HEADS, LANES), 1)


def states_kernel(x_ref, rim_ref, taps_ref, cols_ref, dec_ref, bt_ref,
                  xc_ref, starts_ref, sum_ref, fade_ref, turn_ref, shift_ref):
    rows = x_ref.shape[0]
    segments = rows // SPAN
    turn_ref[...] = turned(cols_ref[...])
    dec = turned(dec_ref[...])
    running = None
    for k in range(segments):
        at = slice(k * SPAN, (k + 1) * SPAN)
        weighted = []
        for j in range(STEP_HEADS):
            lanes = slice(j * LANES, (j + 1) * LANES)
            block = x_ref[at, lanes].astype(f32)
            if k == 0:
                halo = rim_ref[RIM - 8 :, lanes]
            else:
                halo = x_ref[k * SPAN - 16 : k * SPAN, lanes].astype(f32)[8:]
            taps = taps_ref[:, lanes] * 0.5
            shift = shift_ref.at[(k * STEP_HEADS + j) % 2]
            shift[:8] = halo
            shift[8:] = block
            summed = block * taps[3:4]
            for back in range(1, 4):
                summed = summed + shift[8 - back : 8 - back + SPAN] * taps[3 - back : 4 - back]
            xc = half_silu(summed).astype(bf16)
            xc_ref[at, lanes] = xc
            tail = turn_ref[at, 64 + j : 65 + j]
            weighted.append((xc.astype(f32) * tail).astype(bf16))
        fresh = dot(bt_ref[:, at], jnp.concatenate(weighted, axis=1))
        nxt = []
        for j in range(STEP_HEADS):
            piece = fresh[:, j * LANES : (j + 1) * LANES]
            if k > 0:
                starts_ref[k - 1, :, j * LANES : (j + 1) * LANES] = running[j].astype(bf16)
                piece = piece + dec[k : k + 1, j : j + 1] * running[j]
            nxt.append(piece)
        running = nxt
    for j in range(STEP_HEADS):
        sum_ref[j] = running[j].astype(sum_ref.dtype)
        fade_ref[j] = jnp.broadcast_to(dec[segments : segments + 1, j : j + 1], (8, LANES))


def inside(xc_ref, turn_ref, vrow_ref, c_ref, bt_ref, starts_ref, skip_ref, out_ref):
    rows = xc_ref.shape[0]
    segments = rows // SPAN
    half = SPAN // 2
    r = lax.broadcasted_iota(jnp.int32, (half, half), 0)
    c = lax.broadcasted_iota(jnp.int32, (half, half), 1)
    causal = r >= c
    for k in range(segments):
        base = k * SPAN
        at = slice(base, base + SPAN)
        scores = dot(c_ref[at], bt_ref[:, at])
        s_tt = jnp.where(causal, scores[:half, :half], 0.0)
        s_lt = scores[half:, :half]
        s_ll = jnp.where(causal, scores[half:, half:], 0.0)
        if k > 0:
            carried = dot(c_ref[at], starts_ref[k - 1])
        for j in range(STEP_HEADS):
            lanes = slice(j * LANES, (j + 1) * LANES)
            u = turn_ref[at, j : j + 1]
            v = vrow_ref[0, j : j + 1, at]
            m_tt = s_tt * jnp.exp2(jnp.minimum(u[:half] - v[:, :half], 100.0))
            m_lt = s_lt * jnp.exp2(u[half:] - v[:, :half])
            m_ll = s_ll * jnp.exp2(jnp.minimum(u[half:] - v[:, half:], 100.0))
            x = xc_ref[at, lanes]
            y_t = dot(m_tt.astype(bf16), x[:half])
            y_l = dot(jnp.concatenate([m_lt, m_ll], axis=1).astype(bf16), x)
            y = jnp.concatenate([y_t, y_l], axis=0) + skip_ref[pl.program_id(0) * STEP_HEADS + j] * x.astype(f32)
            if k > 0:
                y = y + turn_ref[at, 32 + j : 33 + j] * carried[:, lanes]
            out_ref[at, lanes] = y


def gate(part_ref, z_ref, turn_ref, c_ref, inc_ref, out_ref, sq_ref):
    rows = part_ref.shape[0]
    incoming = jnp.concatenate([inc_ref[j] for j in range(STEP_HEADS)], axis=1)
    for k in range(rows // SPAN):
        at = slice(k * SPAN, (k + 1) * SPAN)
        total = sq_ref[at]
        carried = dot(c_ref[at], incoming)
        for j in range(STEP_HEADS):
            lanes = slice(j * LANES, (j + 1) * LANES)
            mixed = part_ref[at, lanes] + turn_ref[at, 96 + j : 97 + j] * carried[:, lanes]
            gated = mixed * half_silu(z_ref[at, lanes].astype(f32) * 0.5)
            total = total + gated * gated
            out_ref[at, lanes] = gated
        sq_ref[at] = total


def mix_kernel(steps, peers, pairs, inner,
               xc_ref, z_ref, cols_ref, vrow_ref, c_ref, bt_ref, starts_ref, skip_ref,
               sum_ref, fade_ref, init_ref,
               out_ref, inv_ref,
               part_ref, turn_ref, sq_ref, near_ref, near_fade_ref, back_ref, ahead_ref,
               give_ref, inc_ref, now_ref, rows_ref, got_ref,
               near_send, near_recv, fade_send, fade_recv, chain_send, chain_recv,
               give_send, give_recv, sq_send, sq_recv):
    i = pl.program_id(0)
    me = lax.axis_index("seq")
    mine = lax.axis_index("head")
    side = lax.rem(me, 2)
    pair = me // 2
    partner = me + 1 - 2 * side
    chunks = steps // 2
    own = side * chunks
    other = chunks - own

    def to_seq(src, dst, send, recv, target):
        return pltpu.make_async_remote_copy(
            src_ref=src, dst_ref=dst, send_sem=send, recv_sem=recv,
            device_id={"seq": target}, device_id_type=pl.DeviceIdType.MESH)

    def near(c):
        return to_seq(sum_ref.at[pl.ds((other + c) * STEP_HEADS, STEP_HEADS)], near_ref.at[c],
                      near_send.at[c], near_recv.at[c], partner)

    def near_fade():
        return to_seq(fade_ref.at[pl.ds(other * STEP_HEADS, chunks * STEP_HEADS)], near_fade_ref,
                      fade_send, fade_recv, partner)

    def chain(c, target):
        return to_seq(ahead_ref.at[c], back_ref.at[c], chain_send.at[c], chain_recv.at[c], target)

    def give(c):
        return to_seq(give_ref.at[c], inc_ref.at[own + c], give_send.at[c], give_recv.at[c], partner)

    def squares(p):
        return pltpu.make_async_remote_copy(
            src_ref=rows_ref, dst_ref=got_ref.at[p - 1], send_sem=sq_send.at[p - 1],
            recv_sem=sq_recv.at[p - 1], device_id={"head": lax.rem(mine + p, peers)},
            device_id_type=pl.DeviceIdType.MESH)

    @pl.when(i == 0)
    def _():
        barrier = pltpu.get_barrier_semaphore()

        def greet(**where):
            pl.semaphore_signal(barrier, inc=1, device_id=where,
                                device_id_type=pl.DeviceIdType.MESH)

        greet(seq=partner)
        for p in range(1, peers):
            greet(head=lax.rem(mine + p, peers))

        @pl.when(pair > 0)
        def _():
            greet(seq=me - 2)

        @pl.when(pair < pairs - 1)
        def _():
            greet(seq=me + 2)

        pl.semaphore_wait(
            barrier, peers + jnp.minimum(pair, 1) + jnp.minimum(pairs - 1 - pair, 1))
        near_fade().start()
        for c in range(chunks):
            near(c).start()
        sq_ref[...] = jnp.zeros_like(sq_ref)

    def relay(c):
        if c == 0:
            near_fade().wait_recv()
        near(c).wait_recv()

        @pl.when(pair == 0)
        def _():
            for j in range(STEP_HEADS):
                now_ref[j] = init_ref[(own + c) * STEP_HEADS + j].T

        @pl.when(pair > 0)
        def _():
            chain(c, partner).wait_recv()
            now_ref[...] = back_ref[c].astype(f32)

        for j in range(STEP_HEADS):
            h = (own + c) * STEP_HEADS + j
            here, there = sum_ref[h].astype(f32), near_ref[c, j].astype(f32)
            d_here = fade_ref[h][0:1]
            d_there = near_fade_ref[c * STEP_HEADS + j][0:1]
            even = side == 0
            first = now_ref[j]
            second = (jnp.where(even, d_here, d_there) * first
                      + jnp.where(even, here, there))
            last = (jnp.where(even, d_there, d_here) * second
                    + jnp.where(even, there, here))
            inc_ref[own + c, j] = jnp.where(even, first, second).astype(bf16)
            give_ref[c, j] = jnp.where(even, second, first).astype(bf16)
            ahead_ref[c, j] = last.astype(bf16)

        @pl.when(pair < pairs - 1)
        def _():
            chain(c, me + 2).start()

        give(c).start()

    for c in range(chunks):
        pl.when(i == jnp.minimum(RELAY_FROM + c + pair, steps))(functools.partial(relay, c))

    step = lax.rem(i, steps)
    turn_ref[...] = pltpu.roll(cols_ref[...], lax.rem(LANES - step * STEP_HEADS, LANES), 1)

    @pl.when(i < steps)
    def _():
        inside(xc_ref, turn_ref, vrow_ref, c_ref, bt_ref, starts_ref, skip_ref, part_ref.at[step])

    @pl.when(i >= steps)
    def _():
        for c in range(chunks):
            pl.when(step == other + c)(lambda c=c: give(c).wait_recv())
        gate(part_ref.at[step], z_ref, turn_ref, c_ref, inc_ref.at[step], out_ref, sq_ref)

    @pl.when(i == 2 * steps - 1)
    def _():
        count = rows_ref.shape[0]
        for q in range(count):
            rows_ref[q : q + 1] = jnp.sum(sq_ref[q * LANES : (q + 1) * LANES].T, axis=0,
                                          keepdims=True)
        for p in range(1, peers):
            squares(p).start()
        near_fade().wait_send()
        for c in range(chunks):
            near(c).wait_send()
            give(c).wait_send()

        @pl.when(pair < pairs - 1)
        def _():
            for c in range(chunks):
                chain(c, partner).wait_send()

        total = rows_ref[...]
        for p in range(1, peers):
            squares(p).wait_recv()
            total = total + got_ref[p - 1]
        inv_ref[...] = lax.rsqrt(total / inner + norm_eps)
        for p in range(1, peers):
            squares(p).wait_send()


def local(x_input, bc_input, dt_input, z_gate, conv_x, conv_bc, dt_bias, a_log,
          d_skip, init_state, norm_gain, *, inner):
    rows, channels = x_input.shape
    heads = a_log.shape[0]
    state = init_state.shape[2]
    groups = bc_input.shape[2] // state
    steps = heads // STEP_HEADS
    per_group = steps // groups
    width = STEP_HEADS * LANES
    segments = rows // SPAN
    n = lax.axis_size("seq")
    group_cols = bc_input.shape[2]

    params = functools.partial(pltpu.CompilerParams, vmem_limit_bytes=VMEM)
    any_space = pl.BlockSpec(memory_space=pl.ANY)
    in_vmem = pl.BlockSpec(memory_space=pltpu.VMEM)
    dma = pltpu.SemaphoreType.DMA
    cols, vrow, dec, c_mat, b_t, x_rim = pl.pallas_call(
        functools.partial(prepare_kernel, n),
        in_specs=[any_space] + [in_vmem] * 5,
        out_specs=(in_vmem,) * 6,
        out_shape=(
            jax.ShapeDtypeStruct((rows, LANES), f32),
            jax.ShapeDtypeStruct((steps, STEP_HEADS, rows), f32),
            jax.ShapeDtypeStruct((8, LANES), f32),
            jax.ShapeDtypeStruct((rows, group_cols), bf16),
            jax.ShapeDtypeStruct((group_cols, rows), bf16),
            jax.ShapeDtypeStruct((RIM, channels), f32),
        ),
        scratch_shapes=[pltpu.VMEM((RIM, channels), bf16), pltpu.VMEM((2, RIM, group_cols), bf16),
                        pltpu.VMEM((2, RIM, group_cols), f32), dma, dma, dma, dma],
        compiler_params=params(collective_id=1, has_side_effects=True),
        name="prepare",
    )(x_input, dt_input, dt_bias[None], a_log[None], bc_input, conv_bc)

    whole = lambda shape: pl.BlockSpec(shape, lambda i: (0,) * len(shape))
    stripe = pl.BlockSpec((rows, width), lambda i: (0, i))
    bt_spec = pl.BlockSpec((state, rows), lambda i: (i // per_group, 0))
    cols_spec = whole((rows, LANES))
    starts_spec = pl.BlockSpec((segments - 1, state, width), lambda i: (0, 0, i))
    heads_spec = pl.BlockSpec((STEP_HEADS, state, LANES), lambda i: (i, 0, 0))
    x_conv, starts, summary, fade = pl.pallas_call(
        states_kernel,
        grid=(steps,),
        in_specs=[stripe, pl.BlockSpec((RIM, width), lambda i: (0, i)),
                  pl.BlockSpec((4, width), lambda i: (0, i)), cols_spec, whole((8, LANES)), bt_spec],
        out_specs=(stripe, starts_spec, heads_spec,
                   pl.BlockSpec((STEP_HEADS, 8, LANES), lambda i: (i, 0, 0))),
        out_shape=(
            jax.ShapeDtypeStruct((rows, channels), bf16),
            jax.ShapeDtypeStruct((segments - 1, state, channels), bf16),
            jax.ShapeDtypeStruct((heads, state, LANES), bf16),
            jax.ShapeDtypeStruct((heads, 8, LANES), f32),
        ),
        scratch_shapes=[pltpu.VMEM((rows, LANES), f32), pltpu.VMEM((2, SPAN + 8, LANES), f32)],
        compiler_params=params(),
        name="states",
    )(x_input, x_rim, conv_x, cols, dec, b_t)

    chunks = steps // 2
    some = (chunks, STEP_HEADS, state, LANES)
    peers = lax.axis_size("head")
    now = lambda i: lax.rem(i, steps)
    soon = lambda i: jnp.minimum(i, steps - 1)
    late = lambda i: jnp.maximum(i - steps, 0)
    gated, inverse = pl.pallas_call(
        functools.partial(mix_kernel, steps, peers, n // 2, inner),
        grid=(2 * steps,),
        in_specs=[
            pl.BlockSpec((rows, width), lambda i: (0, soon(i))),
            pl.BlockSpec((rows, width), lambda i: (0, late(i))),
            cols_spec,
            pl.BlockSpec((1, STEP_HEADS, rows), lambda i: (soon(i), 0, 0)),
            pl.BlockSpec((rows, state), lambda i: (0, now(i) // per_group)),
            pl.BlockSpec((state, rows), lambda i: (soon(i) // per_group, 0)),
            pl.BlockSpec((segments - 1, state, width), lambda i: (0, 0, soon(i))),
            pl.BlockSpec(memory_space=pltpu.SMEM),
            whole((heads, state, LANES)),
            whole((heads, 8, LANES)),
            whole((heads, LANES, state)),
        ],
        out_specs=(pl.BlockSpec((rows, width), lambda i: (0, late(i))),
                   whole((rows // LANES, LANES))),
        out_shape=(jax.ShapeDtypeStruct((rows, channels), f32),
                   jax.ShapeDtypeStruct((rows // LANES, LANES), f32)),
        scratch_shapes=[
            pltpu.VMEM((steps, rows, width), f32),
            pltpu.VMEM((rows, LANES), f32),
            pltpu.VMEM((rows, LANES), f32),
            pltpu.VMEM(some, bf16),
            pltpu.VMEM((heads // 2, 8, LANES), f32),
            pltpu.VMEM(some, bf16),
            pltpu.VMEM(some, bf16),
            pltpu.VMEM(some, bf16),
            pltpu.VMEM((steps, STEP_HEADS, state, LANES), bf16),
            pltpu.VMEM((STEP_HEADS, state, LANES), f32),
            pltpu.VMEM((rows // LANES, LANES), f32),
            pltpu.VMEM((peers - 1, rows // LANES, LANES), f32),
            dma((chunks,)), dma((chunks,)), dma, dma, dma((chunks,)), dma((chunks,)),
            dma((chunks,)), dma((chunks,)), dma((peers - 1,)), dma((peers - 1,)),
        ],
        compiler_params=params(collective_id=0, has_side_effects=True),
        cost_estimate=pl.CostEstimate(flops=8 * 10**9, bytes_accessed=40 * 2**20, transcendentals=0),
        name="mix",
    )(x_conv, z_gate, cols, vrow, c_mat, b_t, starts, d_skip,
      summary, fade, init_state)
    return (gated * inverse.reshape(rows, 1) * norm_gain).astype(bf16)


def solution(mesh):
    placed = (
        P("seq", "head"), P(None, "seq", "head"), P("seq", "head"), P("seq", "head"),
        P(None, "head"), P(None, None, "head"), P("head"), P("head"), P("head"),
        P("head", None, None), P("head"),
    )

    def run(*args):
        return jax.shard_map(
            functools.partial(local, inner=args[0].shape[1]),
            mesh=mesh, in_specs=placed, out_specs=P("seq", "head"), check_vma=False,
        )(*args)

    return run
```

```python
import functools

import jax
import jax.numpy as jnp
from jax import lax
from jax.experimental import pallas as pl
from jax.experimental.pallas import tpu as pltpu
from jax.sharding import PartitionSpec as P

SPAN = 256
STEP_HEADS = 4
LANES = 128
LOG2E = 1.4426950408889634
RELAY_FROM = 2
RIM = 16
norm_eps = 1e-05
VMEM = 56 * 1024 * 1024
f32 = jnp.float32
bf16 = jnp.bfloat16


def dot(a, b):
    return jnp.dot(a, b, preferred_element_type=f32)


def half_silu(h):
    return h + h * jnp.tanh(h)


def conv_half(halo, block, taps):
    full = jnp.concatenate([halo, block], axis=0)
    acc = block * taps[3:4]
    for back in range(1, 4):
        acc = acc + pltpu.roll(full, back, 0)[8:] * taps[3 - back : 4 - back]
    return acc


def prepare_kernel(count, x_ref, dt_ref, bias_ref, alog_ref, bc_ref, taps_ref,
                   cols_ref, vrow_ref, dec_ref, c_ref, bt_ref, x_rim_ref,
                   x_got_ref, bc_got_ref, bc_rim_ref, x_send, x_recv, bc_send, bc_recv):
    rows = dt_ref.shape[0]
    segments = rows // SPAN
    heads_here = dt_ref.shape[1]
    me = lax.axis_index("seq")
    barrier = pltpu.get_barrier_semaphore()

    def to_next(src, dst, send, recv):
        return pltpu.make_async_remote_copy(
            src_ref=src, dst_ref=dst, send_sem=send, recv_sem=recv,
            device_id={"seq": jnp.minimum(me + 1, count - 1)},
            device_id_type=pl.DeviceIdType.MESH)

    x_copy = to_next(x_ref.at[pl.ds(rows - RIM, RIM)], x_got_ref, x_send, x_recv)
    bc_copy = to_next(bc_ref.at[:, pl.ds(rows - RIM, RIM)], bc_got_ref, bc_send, bc_recv)

    @pl.when(me > 0)
    def _():
        pl.semaphore_signal(barrier, inc=1, device_id={"seq": me - 1},
                            device_id_type=pl.DeviceIdType.MESH)

    @pl.when(me < count - 1)
    def _():
        pl.semaphore_signal(barrier, inc=1, device_id={"seq": me + 1},
                            device_id_type=pl.DeviceIdType.MESH)

    pl.semaphore_wait(barrier, jnp.minimum(me, 1) + jnp.minimum(count - 1 - me, 1))

    @pl.when(me < count - 1)
    def _():
        bc_copy.start()
        x_copy.start()

    rep = (lax.broadcasted_iota(jnp.int32, (heads_here, LANES), 0)
           == lax.broadcasted_iota(jnp.int32, (heads_here, LANES), 1) % heads_here)
    rep = rep.astype(f32)

    def spread(row):
        return jnp.dot(jnp.broadcast_to(row, (8, heads_here)), rep,
                       precision=lax.Precision.HIGHEST, preferred_element_type=f32)[:1]

    r = lax.broadcasted_iota(jnp.int32, (SPAN, SPAN), 0)
    c = lax.broadcasted_iota(jnp.int32, (SPAN, SPAN), 1)
    tri = (r >= c).astype(f32)
    lane = lax.broadcasted_iota(jnp.int32, (SPAN, LANES), 1) // (LANES // 4)
    rate = -jnp.exp(spread(alog_ref[...])) * LOG2E
    bias = spread(bias_ref[...])
    pre = jnp.zeros((1, LANES), f32)
    decays = []
    for k in range(segments):
        at = slice(k * SPAN, (k + 1) * SPAN)
        v = dot(dt_ref[at], rep.astype(bf16)) + bias
        ts = jnp.maximum(v, 0.0) + jnp.log1p(jnp.exp(-jnp.abs(v)))
        cum = jnp.dot(tri, ts * rate, precision=lax.Precision.HIGHEST,
                      preferred_element_type=f32)
        end = cum[SPAN - 1 : SPAN]
        v_rows = (cum - jnp.log2(ts)).T
        for g in range(heads_here // STEP_HEADS):
            vrow_ref[g, :, at] = v_rows[g * STEP_HEADS : (g + 1) * STEP_HEADS]
        tail = jnp.exp2(end - cum) * ts
        cols_ref[at] = jnp.where(
            lane == 0, cum,
            jnp.where(lane == 1, jnp.exp2(cum),
                      jnp.where(lane == 2, tail, jnp.exp2(cum + pre))))
        decays.append(jnp.exp2(end))
        pre = pre + end
    decays.append(jnp.exp2(pre))
    decays.append(jnp.zeros((8 - len(decays), LANES), f32))
    dec_ref[...] = jnp.concatenate(decays, axis=0)

    @pl.when(me > 0)
    def _():
        bc_copy.wait_recv()
        x_copy.wait_recv()
        bc_rim_ref[...] = bc_got_ref[...].astype(f32)
        x_rim_ref[...] = x_got_ref[...].astype(f32)

    @pl.when(me == 0)
    def _():
        bc_rim_ref[...] = jnp.zeros_like(bc_rim_ref)
        x_rim_ref[...] = jnp.zeros_like(x_rim_ref)

    for i in range(2):
        taps = taps_ref[i] * 0.5
        halo = bc_rim_ref[i, RIM - 8 :]
        for k in range(segments):
            at = slice(k * SPAN, (k + 1) * SPAN)
            block = bc_ref[i, at].astype(f32)
            out = half_silu(conv_half(halo, block, taps))
            halo = block[SPAN - 8 :]
            if i == 0:
                bt_ref[:, at] = out.T.astype(bf16)
            else:
                c_ref[at] = out.astype(bf16)

    @pl.when(me < count - 1)
    def _():
        bc_copy.wait_send()
        x_copy.wait_send()


def turned(ref_value, width=LANES):
    step = pl.program_id(0)
    return pltpu.roll(ref_value, lax.rem(LANES - step * STEP_HEADS, LANES), 1)


def states_kernel(x_ref, rim_ref, taps_ref, cols_ref, dec_ref, bt_ref,
                  xc_ref, starts_ref, sum_ref, fade_ref, turn_ref, shift_ref):
    rows = x_ref.shape[0]
    segments = rows // SPAN
    turn_ref[...] = turned(cols_ref[...])
    dec = turned(dec_ref[...])
    running = None
    for k in range(segments):
        at = slice(k * SPAN, (k + 1) * SPAN)
        weighted = []
        for j in range(STEP_HEADS):
            lanes = slice(j * LANES, (j + 1) * LANES)
            block = x_ref[at, lanes].astype(f32)
            if k == 0:
                halo = rim_ref[RIM - 8 :, lanes]
            else:
                halo = x_ref[k * SPAN - 16 : k * SPAN, lanes].astype(f32)[8:]
            taps = taps_ref[:, lanes] * 0.5
            shift = shift_ref.at[(k * STEP_HEADS + j) % 2]
            shift[:8] = halo
            shift[8:] = block
            summed = block * taps[3:4]
            for back in range(1, 4):
                summed = summed + shift[8 - back : 8 - back + SPAN] * taps[3 - back : 4 - back]
            xc = half_silu(summed).astype(bf16)
            xc_ref[at, lanes] = xc
            tail = turn_ref[at, 64 + j : 65 + j]
            weighted.append((xc.astype(f32) * tail).astype(bf16))
        fresh = dot(bt_ref[:, at], jnp.concatenate(weighted, axis=1))
        nxt = []
        for j in range(STEP_HEADS):
            piece = fresh[:, j * LANES : (j + 1) * LANES]
            if k > 0:
                starts_ref[k - 1, :, j * LANES : (j + 1) * LANES] = running[j].astype(bf16)
                piece = piece + dec[k : k + 1, j : j + 1] * running[j]
            nxt.append(piece)
        running = nxt
    for j in range(STEP_HEADS):
        sum_ref[j] = running[j].astype(sum_ref.dtype)
        fade_ref[j] = jnp.broadcast_to(dec[segments : segments + 1, j : j + 1], (8, LANES))


def inside(xc_ref, turn_ref, vrow_ref, c_ref, bt_ref, starts_ref, skip_ref, out_ref):
    rows = xc_ref.shape[0]
    segments = rows // SPAN
    half = SPAN // 2
    r = lax.broadcasted_iota(jnp.int32, (half, half), 0)
    c = lax.broadcasted_iota(jnp.int32, (half, half), 1)
    causal = r >= c
    for k in range(segments):
        base = k * SPAN
        at = slice(base, base + SPAN)
        scores = dot(c_ref[at], bt_ref[:, at])
        s_tt = jnp.where(causal, scores[:half, :half], 0.0)
        s_lt = scores[half:, :half]
        s_ll = jnp.where(causal, scores[half:, half:], 0.0)
        if k > 0:
            carried = dot(c_ref[at], starts_ref[k - 1])
        for j in range(STEP_HEADS):
            lanes = slice(j * LANES, (j + 1) * LANES)
            u = turn_ref[at, j : j + 1]
            v = vrow_ref[0, j : j + 1, at]
            m_tt = s_tt * jnp.exp2(jnp.minimum(u[:half] - v[:, :half], 100.0))
            m_lt = s_lt * jnp.exp2(u[half:] - v[:, :half])
            m_ll = s_ll * jnp.exp2(jnp.minimum(u[half:] - v[:, half:], 100.0))
            x = xc_ref[at, lanes]
            y_t = dot(m_tt.astype(bf16), x[:half])
            y_l = dot(jnp.concatenate([m_lt, m_ll], axis=1).astype(bf16), x)
            y = jnp.concatenate([y_t, y_l], axis=0) + skip_ref[pl.program_id(0) * STEP_HEADS + j] * x.astype(f32)
            if k > 0:
                y = y + turn_ref[at, 32 + j : 33 + j] * carried[:, lanes]
            out_ref[at, lanes] = y


def gate(part_ref, z_ref, turn_ref, c_ref, inc_ref, out_ref, sq_ref):
    rows = part_ref.shape[0]
    incoming = jnp.concatenate([inc_ref[j] for j in range(STEP_HEADS)], axis=1)
    for k in range(rows // SPAN):
        at = slice(k * SPAN, (k + 1) * SPAN)
        total = sq_ref[at]
        carried = dot(c_ref[at], incoming)
        for j in range(STEP_HEADS):
            lanes = slice(j * LANES, (j + 1) * LANES)
            mixed = part_ref[at, lanes] + turn_ref[at, 96 + j : 97 + j] * carried[:, lanes]
            gated = mixed * half_silu(z_ref[at, lanes].astype(f32) * 0.5)
            total = total + gated * gated
            out_ref[at, lanes] = gated
        sq_ref[at] = total


def turn_of(i, steps):
    own = lax.rem(lax.axis_index("seq"), 2) * (steps // 2)
    late = jnp.minimum(i // steps, 1)
    return lax.rem(i + late * own, steps)


def mix_kernel(steps, peers, pairs, inner,
               xc_ref, z_ref, cols_ref, vrow_ref, c_ref, bt_ref, starts_ref, skip_ref,
               sum_ref, fade_ref, init_ref,
               out_ref, inv_ref,
               part_ref, turn_ref, sq_ref, near_ref, near_fade_ref, back_ref, ahead_ref,
               give_ref, inc_ref, now_ref, rows_ref, got_ref,
               near_send, near_recv, fade_send, fade_recv, chain_send, chain_recv,
               give_send, give_recv, sq_send, sq_recv):
    i = pl.program_id(0)
    me = lax.axis_index("seq")
    mine = lax.axis_index("head")
    side = lax.rem(me, 2)
    pair = me // 2
    partner = me + 1 - 2 * side
    chunks = steps // 2
    own = side * chunks
    other = chunks - own

    def to_seq(src, dst, send, recv, target):
        return pltpu.make_async_remote_copy(
            src_ref=src, dst_ref=dst, send_sem=send, recv_sem=recv,
            device_id={"seq": target}, device_id_type=pl.DeviceIdType.MESH)

    def near(c):
        return to_seq(sum_ref.at[pl.ds((other + c) * STEP_HEADS, STEP_HEADS)], near_ref.at[c],
                      near_send.at[c], near_recv.at[c], partner)

    def near_fade():
        return to_seq(fade_ref.at[pl.ds(other * STEP_HEADS, chunks * STEP_HEADS)], near_fade_ref,
                      fade_send, fade_recv, partner)

    def chain(c, target):
        return to_seq(ahead_ref.at[c], back_ref.at[c], chain_send.at[c], chain_recv.at[c], target)

    def give(c):
        return to_seq(give_ref.at[c], inc_ref.at[own + c], give_send.at[c], give_recv.at[c], partner)

    def squares(p):
        return pltpu.make_async_remote_copy(
            src_ref=rows_ref, dst_ref=got_ref.at[p - 1], send_sem=sq_send.at[p - 1],
            recv_sem=sq_recv.at[p - 1], device_id={"head": lax.rem(mine + p, peers)},
            device_id_type=pl.DeviceIdType.MESH)

    @pl.when(i == 0)
    def _():
        barrier = pltpu.get_barrier_semaphore()

        def greet(**where):
            pl.semaphore_signal(barrier, inc=1, device_id=where,
                                device_id_type=pl.DeviceIdType.MESH)

        greet(seq=partner)
        for p in range(1, peers):
            greet(head=lax.rem(mine + p, peers))

        @pl.when(pair > 0)
        def _():
            greet(seq=me - 2)

        @pl.when(pair < pairs - 1)
        def _():
            greet(seq=me + 2)

        pl.semaphore_wait(
            barrier, peers + jnp.minimum(pair, 1) + jnp.minimum(pairs - 1 - pair, 1))
        near_fade().start()
        for c in range(chunks):
            near(c).start()
        sq_ref[...] = jnp.zeros_like(sq_ref)

    def relay(c):
        if c == 0:
            near_fade().wait_recv()
        near(c).wait_recv()

        @pl.when(pair == 0)
        def _():
            for j in range(STEP_HEADS):
                now_ref[j] = init_ref[(own + c) * STEP_HEADS + j].T

        @pl.when(pair > 0)
        def _():
            chain(c, partner).wait_recv()
            now_ref[...] = back_ref[c].astype(f32)

        for j in range(STEP_HEADS):
            h = (own + c) * STEP_HEADS + j
            here, there = sum_ref[h].astype(f32), near_ref[c, j].astype(f32)
            d_here = fade_ref[h][0:1]
            d_there = near_fade_ref[c * STEP_HEADS + j][0:1]
            even = side == 0
            first = now_ref[j]
            second = (jnp.where(even, d_here, d_there) * first
                      + jnp.where(even, here, there))
            last = (jnp.where(even, d_there, d_here) * second
                    + jnp.where(even, there, here))
            inc_ref[own + c, j] = jnp.where(even, first, second).astype(bf16)
            give_ref[c, j] = jnp.where(even, second, first).astype(bf16)
            ahead_ref[c, j] = last.astype(bf16)

        @pl.when(pair < pairs - 1)
        def _():
            chain(c, me + 2).start()

        give(c).start()

    for c in range(chunks):
        pl.when(i == jnp.minimum(RELAY_FROM + c + 2 * pair, steps + c))(functools.partial(relay, c))

    step = turn_of(i, steps)
    turn_ref[...] = pltpu.roll(cols_ref[...], lax.rem(LANES - step * STEP_HEADS, LANES), 1)

    @pl.when(i < steps)
    def _():
        inside(xc_ref, turn_ref, vrow_ref, c_ref, bt_ref, starts_ref, skip_ref, part_ref.at[step])

    @pl.when(i >= steps)
    def _():
        for c in range(chunks):
            pl.when(step == other + c)(lambda c=c: give(c).wait_recv())
        gate(part_ref.at[step], z_ref, turn_ref, c_ref, inc_ref.at[step], out_ref, sq_ref)

    @pl.when(i == 2 * steps - 1)
    def _():
        count = rows_ref.shape[0]
        for q in range(count):
            rows_ref[q : q + 1] = jnp.sum(sq_ref[q * LANES : (q + 1) * LANES].T, axis=0,
                                          keepdims=True)
        for p in range(1, peers):
            squares(p).start()
        near_fade().wait_send()
        for c in range(chunks):
            near(c).wait_send()
            give(c).wait_send()

        @pl.when(pair < pairs - 1)
        def _():
            for c in range(chunks):
                chain(c, partner).wait_send()

        total = rows_ref[...]
        for p in range(1, peers):
            squares(p).wait_recv()
            total = total + got_ref[p - 1]
        inv_ref[...] = lax.rsqrt(total / inner + norm_eps)
        for p in range(1, peers):
            squares(p).wait_send()


def local(x_input, bc_input, dt_input, z_gate, conv_x, conv_bc, dt_bias, a_log,
          d_skip, init_state, norm_gain, *, inner):
    rows, channels = x_input.shape
    heads = a_log.shape[0]
    state = init_state.shape[2]
    groups = bc_input.shape[2] // state
    steps = heads // STEP_HEADS
    per_group = steps // groups
    width = STEP_HEADS * LANES
    segments = rows // SPAN
    n = lax.axis_size("seq")
    group_cols = bc_input.shape[2]

    params = functools.partial(pltpu.CompilerParams, vmem_limit_bytes=VMEM)
    any_space = pl.BlockSpec(memory_space=pl.ANY)
    in_vmem = pl.BlockSpec(memory_space=pltpu.VMEM)
    dma = pltpu.SemaphoreType.DMA
    cols, vrow, dec, c_mat, b_t, x_rim = pl.pallas_call(
        functools.partial(prepare_kernel, n),
        in_specs=[any_space] + [in_vmem] * 5,
        out_specs=(in_vmem,) * 6,
        out_shape=(
            jax.ShapeDtypeStruct((rows, LANES), f32),
            jax.ShapeDtypeStruct((steps, STEP_HEADS, rows), f32),
            jax.ShapeDtypeStruct((8, LANES), f32),
            jax.ShapeDtypeStruct((rows, group_cols), bf16),
            jax.ShapeDtypeStruct((group_cols, rows), bf16),
            jax.ShapeDtypeStruct((RIM, channels), f32),
        ),
        scratch_shapes=[pltpu.VMEM((RIM, channels), bf16), pltpu.VMEM((2, RIM, group_cols), bf16),
                        pltpu.VMEM((2, RIM, group_cols), f32), dma, dma, dma, dma],
        compiler_params=params(collective_id=1, has_side_effects=True),
        name="prepare",
    )(x_input, dt_input, dt_bias[None], a_log[None], bc_input, conv_bc)

    whole = lambda shape: pl.BlockSpec(shape, lambda i: (0,) * len(shape))
    stripe = pl.BlockSpec((rows, width), lambda i: (0, i))
    bt_spec = pl.BlockSpec((state, rows), lambda i: (i // per_group, 0))
    cols_spec = whole((rows, LANES))
    starts_spec = pl.BlockSpec((segments - 1, state, width), lambda i: (0, 0, i))
    heads_spec = pl.BlockSpec((STEP_HEADS, state, LANES), lambda i: (i, 0, 0))
    x_conv, starts, summary, fade = pl.pallas_call(
        states_kernel,
        grid=(steps,),
        in_specs=[stripe, pl.BlockSpec((RIM, width), lambda i: (0, i)),
                  pl.BlockSpec((4, width), lambda i: (0, i)), cols_spec, whole((8, LANES)), bt_spec],
        out_specs=(stripe, starts_spec, heads_spec,
                   pl.BlockSpec((STEP_HEADS, 8, LANES), lambda i: (i, 0, 0))),
        out_shape=(
            jax.ShapeDtypeStruct((rows, channels), bf16),
            jax.ShapeDtypeStruct((segments - 1, state, channels), bf16),
            jax.ShapeDtypeStruct((heads, state, LANES), bf16),
            jax.ShapeDtypeStruct((heads, 8, LANES), f32),
        ),
        scratch_shapes=[pltpu.VMEM((rows, LANES), f32), pltpu.VMEM((2, SPAN + 8, LANES), f32)],
        compiler_params=params(),
        name="states",
    )(x_input, x_rim, conv_x, cols, dec, b_t)

    chunks = steps // 2
    some = (chunks, STEP_HEADS, state, LANES)
    peers = lax.axis_size("head")
    now = lambda i: turn_of(i, steps)
    soon = lambda i: jnp.minimum(i, steps - 1)
    late = lambda i: turn_of(jnp.maximum(i, steps), steps)
    gated, inverse = pl.pallas_call(
        functools.partial(mix_kernel, steps, peers, n // 2, inner),
        grid=(2 * steps,),
        in_specs=[
            pl.BlockSpec((rows, width), lambda i: (0, soon(i))),
            pl.BlockSpec((rows, width), lambda i: (0, late(i))),
            cols_spec,
            pl.BlockSpec((1, STEP_HEADS, rows), lambda i: (soon(i), 0, 0)),
            pl.BlockSpec((rows, state), lambda i: (0, now(i) // per_group)),
            pl.BlockSpec((state, rows), lambda i: (soon(i) // per_group, 0)),
            pl.BlockSpec((segments - 1, state, width), lambda i: (0, 0, soon(i))),
            pl.BlockSpec(memory_space=pltpu.SMEM),
            whole((heads, state, LANES)),
            whole((heads, 8, LANES)),
            whole((heads, LANES, state)),
        ],
        out_specs=(pl.BlockSpec((rows, width), lambda i: (0, late(i))),
                   whole((rows // LANES, LANES))),
        out_shape=(jax.ShapeDtypeStruct((rows, channels), f32),
                   jax.ShapeDtypeStruct((rows // LANES, LANES), f32)),
        scratch_shapes=[
            pltpu.VMEM((steps, rows, width), f32),
            pltpu.VMEM((rows, LANES), f32),
            pltpu.VMEM((rows, LANES), f32),
            pltpu.VMEM(some, bf16),
            pltpu.VMEM((heads // 2, 8, LANES), f32),
            pltpu.VMEM(some, bf16),
            pltpu.VMEM(some, bf16),
            pltpu.VMEM(some, bf16),
            pltpu.VMEM((steps, STEP_HEADS, state, LANES), bf16),
            pltpu.VMEM((STEP_HEADS, state, LANES), f32),
            pltpu.VMEM((rows // LANES, LANES), f32),
            pltpu.VMEM((peers - 1, rows // LANES, LANES), f32),
            dma((chunks,)), dma((chunks,)), dma, dma, dma((chunks,)), dma((chunks,)),
            dma((chunks,)), dma((chunks,)), dma((peers - 1,)), dma((peers - 1,)),
        ],
        compiler_params=params(collective_id=0, has_side_effects=True),
        cost_estimate=pl.CostEstimate(flops=8 * 10**9, bytes_accessed=40 * 2**20, transcendentals=0),
        name="mix",
    )(x_conv, z_gate, cols, vrow, c_mat, b_t, starts, d_skip,
      summary, fade, init_state)
    return (gated * inverse.reshape(rows, 1) * norm_gain).astype(bf16)


def solution(mesh):
    placed = (
        P("seq", "head"), P(None, "seq", "head"), P("seq", "head"), P("seq", "head"),
        P(None, "head"), P(None, None, "head"), P("head"), P("head"), P("head"),
        P("head", None, None), P("head"),
    )

    def run(*args):
        return jax.shard_map(
            functools.partial(local, inner=args[0].shape[1]),
            mesh=mesh, in_specs=placed, out_specs=P("seq", "head"), check_vma=False,
        )(*args)

    return run
```
